32 devices in a mesh: dp: 8 (over z, x), tensor: 4 (over y, core).
Axes of the slice: x: 2, y: 2, z: 4, core: 2. Of those that a mesh axis runs over, the one named last changes fastest.
Arguments:
- activations: bfloat16 [2048, 768], P('dp', 'tensor'), may hold values from -6 to 6
- output_grad: bfloat16 [2048, 768], P('dp', 'tensor'), may hold values from -6 to 6
- seq_lengths: int32 [16], P('dp'), may hold values from 0 to 256, as said below
- routes: int32 [2048, 1], P('dp'), may hold values from 0 to 7; in each aligned block of 256 rows (0 to 255, 256 to 511, ...) at most 36 rows name the same one
- buckets: int32 [256], replicated, may hold values from 0 to 31
- norm1_gain: bfloat16 [768], P('tensor'), may hold values from 0.5 to 1.5
- w_query: bfloat16 [768, 768], P(None, 'tensor'), may hold values from -0.21875 to 0.21875
- w_key: bfloat16 [768, 768], P(None, 'tensor'), may hold values from -0.21875 to 0.21875
- w_value: bfloat16 [768, 768], P(None, 'tensor'), may hold values from -0.21875 to 0.21875
- w_output: bfloat16 [768, 768], P('tensor'), may hold values from -1.25 to 1.25
- bias_table: bfloat16 [32, 12], P(None, 'tensor'), may hold values from -4 to 4
- norm2_gain: bfloat16 [768], replicated, may hold values from 0.5 to 1.5
- w_router: bfloat16 [768, 8], replicated, may hold values from -0.15625 to 0.15625
- w_in: bfloat16 [8, 768, 3072], P('dp', None, 'tensor'), may hold values from -0.21875 to 0.21875
- w_out: bfloat16 [8, 3072, 768], P('dp', 'tensor'), may hold values from -1.25 to 1.25
Outputs:
- block_output: bfloat16 [2048, 768], P('dp', 'tensor')
- input_grad: float32 [2048, 768], P('dp', 'tensor')
- grad_norm1_gain: float32 [768], P('tensor')
- grad_w_query: float32 [768, 768], P(None, 'tensor')
- grad_w_key: float32 [768, 768], P(None, 'tensor')
- grad_w_value: float32 [768, 768], P(None, 'tensor')
- grad_w_output: float32 [768, 768], P('tensor')
- grad_bias_table: float32 [32, 12], P(None, 'tensor')
- grad_norm2_gain: float32 [768], replicated
- grad_w_router: float32 [768, 8], replicated
- grad_w_in: float32 [8, 768, 3072], P('dp', None, 'tensor')
- grad_w_out: float32 [8, 3072, 768], P('dp', 'tensor')
The draws below stay inside these ranges and needn't reach their ends.
Inputs may be any that keep to these rules, and one draw needn't show every extreme that they name: `seq_lengths`: entries 2 d and 2 d + 1 are the lengths of the two sequences of index d of dp, placed from its first row in that order; 0 marks an empty second place. The two lengths of a device sum to at most 256, every nonzero length is at least min(48, 256), and some device holds one sequence of exactly 256 tokens. `routes`: routes of unused rows are not read. Among the 256 rows of one device at most 36 name the same expert, a bound that some block reaches.
All inputs are finite; a program needn't handle non-finite values.
Results may differ from the reference program's by a relative error of at most 0.025.
Values may be sent and summed in bfloat16 or wider, within the bound.
A program may use at most 64 MiB of HBM per device.

```python
import math
import jax
import jax.numpy as jnp
import numpy as np
from jax import lax

D = 768
H = 12
DH = 64
FF = 3072
NB = 32
CAP = 256
LMIN = 48
EXPERTS = 8
CAPX = 36
TOKENS = 2048
N_DP = 8
N_TENSOR = 4


def draw_seq_lengths(key, part):
    key = jax.random.fold_in(key, 7)
    first_key, second_key, full_key = jax.random.split(key, 3)
    shortest = min(LMIN, CAP)
    first_len = jax.random.randint(first_key, (N_DP,), shortest, CAP + 1)
    second_len = jax.random.randint(second_key, (N_DP,), 0, CAP - first_len + 1)
    second_len = jnp.where(second_len < shortest, 0, second_len)
    fullest = jax.random.randint(full_key, (), 0, N_DP)
    devices_index = jnp.arange(N_DP)
    first_len = jnp.where(devices_index == fullest, CAP, first_len)
    second_len = jnp.where(devices_index == fullest, 0, second_len)
    return jnp.stack([first_len, second_len], axis=1).reshape(2 * N_DP).astype(jnp.int32)


def plant(values, key, low, largest):
    longest = values.shape.index(max(values.shape))
    spots = []
    for shift in (0, 1):
        where = [jax.random.randint(jax.random.fold_in(key, axis), (), 0, length) for axis, length in enumerate(values.shape)]
        where[longest] = (where[longest] + shift) % values.shape[longest]
        spots.append(tuple(where))
    return values.at[spots[0]].set(low).at[spots[1]].set(largest)


def levels(stream_key, shape, cuts, smallest, largest):
    factor_of, own = 1.0, jax.random.fold_in(stream_key, 6)
    for dim, blocks in cuts:
        steps = jnp.exp(jax.random.uniform(jax.random.fold_in(own, dim), (blocks,), jnp.float32, smallest / len(cuts), largest / len(cuts)))
        factor_of = factor_of * jnp.repeat(steps, shape[dim] // blocks).reshape([-1 if axis == dim else 1 for axis in range(len(shape))])
    return factor_of


def assign_block(key, own, number, rows, count, top, most, skew):
    order = jax.random.permutation(key, count)
    crowded, common = shares(count, rows * top, most, skew, True), shares(count, rows * top, most, skew, False)
    places = jnp.arange(count)

    def named(sizes, rotation):
        used = int((sizes > 0).sum())
        fixed = max(1, used // 4)
        moved = fixed + (places - fixed + rotation * (used - fixed)) % max(1, count - fixed)
        return jnp.zeros((count,), jnp.int32).at[order[jnp.where(places < fixed, places, moved)]].set(jnp.asarray(sizes, jnp.int32))

    sizes = jnp.where(number % 4 == 0, named(crowded, number // 4), named(common, number - number // 4 - 1))
    mixed = jax.random.permutation(jax.random.fold_in(own, 3), count)
    source_of, sink = mixed[0:count // 2 * 2:2], mixed[1:count // 2 * 2:2]
    room = jnp.minimum(sizes[source_of] - 1, most - sizes[sink]) // 2
    room = jnp.where((source_of == order[0]) | (sink == order[0]) | (sizes[sink] == 0), 0, jnp.maximum(room, 0))
    moved = jax.random.randint(jax.random.fold_in(own, 4), (count // 2,), 0, 1 << 20) % (room + 1)
    sizes = sizes.at[source_of].add(-moved).at[sink].add(moved)
    items = jnp.searchsorted(jnp.cumsum(sizes), jnp.arange(rows * top), side="right").astype(jnp.int32)
    grid = items.reshape(top, rows).T
    grid = grid[jax.random.permutation(jax.random.fold_in(own, 1), rows)]
    rotation = jax.random.randint(jax.random.fold_in(own, 2), (rows, 1), 0, top)
    return jnp.take_along_axis(grid, (jnp.arange(top)[None, :] + rotation) % top, axis=1)


def shares(amount, total, reach, slope, full):
    weights = [(1 << 20) // math.isqrt(standing ** slope) + 1 for standing in range(1, amount + 1)]
    largest = reach if full else min(reach, max(-(-total // amount), total * weights[0] // sum(weights)))
    least = 1 if total - largest >= amount - 1 else 0
    holding, surplus = [largest] + [least] * (amount - 1), total - largest - least * (amount - 1)
    while surplus > 0:
        free = [i for i in range(1, amount) if holding[i] < largest] or [i for i in range(1, amount) if holding[i] < reach]
        mass, budget = sum([weights[i] for i in free]), surplus
        for i in free:
            extra = min(reach - holding[i], max(1, budget * weights[i] // mass), surplus)
            holding[i] = holding[i] + extra
            surplus = surplus - extra
    return np.array(holding)


def centred(rng, extent, width, limit, cuts=(), held_as=jnp.bfloat16):
    result = width * jax.random.normal(rng, extent, jnp.float32)
    if cuts:
        result = result * levels(rng, extent, cuts, -0.22, 0.18)
    return jnp.clip(result, -limit, limit).astype(held_as)


def setup_inputs(seed: int = 0) -> dict:
    key_list = jax.random.split(jax.random.key(seed), 16)
    activations = centred(key_list[0], (TOKENS, D), 1.0, 6.0, ((0, 8), (1, 4)))
    output_grad = centred(key_list[1], (TOKENS, D), 1.0, 6.0, ((0, 8), (1, 4)))
    seq_lengths = draw_seq_lengths(jax.random.fold_in(key_list[15], 71), 0)
    routes_keys = jax.random.split(jax.random.fold_in(key_list[3], 1), TOKENS // CAP)
    routes_turns = jax.random.permutation(jax.random.fold_in(key_list[3], 3), TOKENS // CAP)
    routes = jax.vmap(lambda own, number: assign_block(jax.random.fold_in(key_list[3], 2), own, number, CAP, EXPERTS, 1, CAPX, 1))(routes_keys, routes_turns).reshape((TOKENS, 1))
    buckets = plant(jax.random.randint(key_list[4], (CAP,), 0, NB), jax.random.fold_in(key_list[4], 1), 0, NB - 1).astype(jnp.int32)
    norm1_gain = jnp.clip(1.0 + 0.1 * jax.random.normal(key_list[5], (D,), jnp.float32), 0.5, 1.5).astype(jnp.bfloat16)
    w_query = centred(key_list[6], (D, H * DH), D ** -0.5, 0.21875, ((1, 4),))
    w_key = centred(key_list[7], (D, H * DH), D ** -0.5, 0.21875, ((1, 4),))
    w_value = centred(key_list[8], (D, H * DH), D ** -0.5, 0.21875, ((1, 4),))
    w_output = centred(key_list[9], (H * DH, D), (H * DH // 32) ** -0.5, 1.25, ((0, 4),))
    bias_table = centred(key_list[10], (NB, H), 1.0, 4.0, ((1, 4),))
    norm2_gain = jnp.clip(1.0 + 0.1 * jax.random.normal(key_list[11], (D,), jnp.float32), 0.5, 1.5).astype(jnp.bfloat16)
    w_router = centred(key_list[12], (D, EXPERTS), (2 * D) ** -0.5, 0.15625)
    w_in = centred(key_list[13], (EXPERTS, D, FF), D ** -0.5, 0.21875, ((0, 8), (2, 4)))
    w_out = centred(key_list[14], (EXPERTS, FF, D), (1.5 * EXPERTS * FF ** -0.5), 1.25, ((0, 8), (1, 4)))
    return {"activations": activations, "output_grad": output_grad, "seq_lengths": seq_lengths, "routes": routes, "buckets": buckets, "norm1_gain": norm1_gain, "w_query": w_query, "w_key": w_key, "w_value": w_value, "w_output": w_output, "bias_table": bias_table, "norm2_gain": norm2_gain, "w_router": w_router, "w_in": w_in, "w_out": w_out}


EPSILON = 1e-06
NEGATIVE = -1e+30
HIGHEST = lax.Precision.HIGHEST

@jax.custom_vjp
def low(v):
    return lax.optimization_barrier(v.astype(jnp.bfloat16)).astype(jnp.float32)

@jax.custom_vjp
def low_back(v):
    return v

def low_keep(v):
    return (low(v), None)

def low_pass(kept, grad):
    return (grad,)

def back_keep(v):
    return (v, None)

def back_low(kept, grad):
    return (low(grad),)
low.defvjp(low_keep, low_pass)
low_back.defvjp(back_keep, back_low)

def product(left, right):
    return jnp.dot(left, right, precision=HIGHEST)

def normalize(values, gain):
    return values * lax.rsqrt(lax.optimization_barrier(jnp.mean(values * values, axis=-1, keepdims=True)) + EPSILON) * gain

def reference(activations, output_grad, seq_lengths, routes, buckets, norm1_gain, w_query, w_key, w_value, w_output, bias_table, norm2_gain, w_router, w_in, w_out):
    position = jnp.arange(CAP, dtype=jnp.int32)
    lengths = seq_lengths.reshape(N_DP, 2).astype(jnp.int32)
    first_len = lengths[:, 0:1]
    second_len = lengths[:, 1:2]
    segment = jnp.where(position[None, :] < first_len, 0, jnp.where(position[None, :] < first_len + second_len, 1, 2)).astype(jnp.int32)
    live_mask = segment < 2
    live = live_mask.reshape(TOKENS, 1).astype(jnp.float32)
    expert_id = routes[:, 0].reshape(N_DP, CAP).astype(jnp.int32)
    picked = (expert_id[:, :, None] == jnp.arange(EXPERTS, dtype=jnp.int32)[None, None, :]) & live_mask[:, :, None]
    earlier = jnp.cumsum(picked.astype(jnp.int32), axis=1) - 1
    slot_rank = lax.optimization_barrier(jnp.sum(jnp.where(picked, earlier, 0), axis=2)).astype(jnp.int32)
    per_expert = N_DP * CAPX
    slot_global = (expert_id * per_expert + jnp.arange(N_DP, dtype=jnp.int32)[:, None] * CAPX + slot_rank).reshape(TOKENS).astype(jnp.int32)
    live_flat = live_mask.reshape(TOKENS)
    target = jnp.where(live_flat, slot_global, EXPERTS * per_expert).astype(jnp.int32)
    token_of_slot = jnp.full((EXPERTS * per_expert,), TOKENS, jnp.int32).at[target].set(jnp.arange(TOKENS, dtype=jnp.int32), mode='drop')
    slot_filled = (token_of_slot < TOKENS).astype(jnp.float32)[:, None]
    slot_source = jnp.minimum(token_of_slot, TOKENS - 1).astype(jnp.int32)
    slot_taken = jnp.where(live_flat, slot_global, 0).astype(jnp.int32)
    route_onehot = (routes[:, 0:1].astype(jnp.int32) == jnp.arange(EXPERTS, dtype=jnp.int32)[None, :]).astype(jnp.float32)
    relative = position[:, None] - position[None, :]
    causal = relative >= 0
    bucket_grid = buckets.astype(jnp.int32)[jnp.clip(relative, 0, CAP - 1)]
    group_heads = H // N_TENSOR
    group_units = FF // N_TENSOR

    def forward(x_rows, gain_one, query_w, key_w, value_w, output_w, table_w, gain_two, router_w, inner_w, outer_w):
        normed_one = low(normalize(x_rows, gain_one))
        query = low(low_back(product(normed_one, query_w))).reshape(N_DP, CAP, H, DH)
        key = low(low_back(product(normed_one, key_w))).reshape(N_DP, CAP, H, DH)
        value = low(low_back(product(normed_one, value_w))).reshape(N_DP, CAP, H, DH)

        def attend(pieces):
            query_rows, key_rows, value_rows, segment_rows = pieces
            bias_grid = jnp.transpose(table_w[bucket_grid], (2, 0, 1))
            scores = jnp.einsum('ihd,jhd->hij', query_rows, key_rows, precision=HIGHEST) * DH ** (-0.5) + bias_grid
            scores = low_back(scores)
            allowed = causal & (segment_rows[:, None] == segment_rows[None, :])
            weights = low(jax.nn.softmax(jnp.where(allowed[None], scores, NEGATIVE), axis=-1))
            heads_out = low(low_back(jnp.einsum('hij,jhd->ihd', weights, value_rows, precision=HIGHEST)))
            grouped = heads_out.reshape(CAP, N_TENSOR, group_heads * DH)
            part_sums = jnp.einsum('itc,tcd->itd', grouped, output_w.reshape(N_TENSOR, group_heads * DH, D), precision=HIGHEST)
            return low_back(lax.optimization_barrier(jnp.sum(low(part_sums), axis=1)))
        attn_rows = lax.map(jax.checkpoint(attend), (query, key, value, segment)).reshape(TOKENS, D)
        hidden = x_rows + live * attn_rows
        normed_two = low(normalize(hidden, gain_two))
        logits = low_back(product(normed_two, router_w))
        gate_value = lax.optimization_barrier(jnp.sum(jax.nn.softmax(logits, axis=-1) * route_onehot, axis=1, keepdims=True))
        routed = low_back(normed_two)
        expert_rows = (jnp.take(routed, slot_source, axis=0) * slot_filled).reshape(EXPERTS, per_expert, D)

        def expert(pieces):
            expert_input, inner_one, outer_one = pieces
            pre_act = low_back(product(expert_input, inner_one))
            activated = low(jax.nn.gelu(pre_act))
            part_sums = jnp.einsum('rtf,tfd->rtd', activated.reshape(per_expert, N_TENSOR, group_units), outer_one.reshape(N_TENSOR, group_units, D), precision=HIGHEST)
            return low(low_back(lax.optimization_barrier(jnp.sum(low(part_sums), axis=1))))
        returned = lax.map(jax.checkpoint(expert), (expert_rows, inner_w, outer_w)).reshape(EXPERTS * per_expert, D)
        moe_rows = jnp.take(returned, slot_taken, axis=0)
        return hidden + live * gate_value * moe_rows
    inputs = tuple((argument.astype(jnp.float32) for argument in (activations, norm1_gain, w_query, w_key, w_value, w_output, bias_table, norm2_gain, w_router, w_in, w_out)))
    output, pullback = jax.vjp(forward, *inputs)
    gradients = pullback(output_grad.astype(jnp.float32))
    return (output.astype(jnp.bfloat16), gradients[0], gradients[1], gradients[2], gradients[3], gradients[4], gradients[5], gradients[6], gradients[7], gradients[8], gradients[9], gradients[10])
```

```python
import functools
import math

import jax
import jax.numpy as jnp
from jax import lax
from jax.experimental import pallas as pl
from jax.experimental.pallas import tpu as pltpu
from jax.sharding import PartitionSpec as P

DH = 64
EPSILON = 1e-06
NEGATIVE = -1e30
F32 = jnp.float32
BF16 = jnp.bfloat16
MESH = pl.DeviceIdType.MESH


def dot(left, right, left_axis=1, right_axis=0):
    return lax.dot_general(
        left, right, (((left_axis,), (right_axis,)), ((), ())), preferred_element_type=F32
    )


def iota(shape, axis):
    return lax.broadcasted_iota(jnp.int32, shape, axis)


def kernel(
    n_dp, n_t, slots, pad,
    lens_ref, x_ref, dy_ref, routes_ref, buckets_ref, gain1_ref, wq_ref, wk_ref, wv_ref, wo_ref,
    table_ref, gain2_ref, wr_ref, win_ref, wout_ref,
    out_ref, dx_ref, dgain1_ref, dwq_ref, dwk_ref, dwv_ref, dwo_ref, dtable_ref, dgain2_ref,
    dwr_ref, dwin_ref, dwout_ref,
    xs, gs, a_send, a_recv, a_sum, sent, arrived, parts, parts_in, back, back_in,
    eg_all, row_part, row_in, one_send, one_in, row2_part, row2_in,
    grads, grads_in, grads_all, small1, small2, small1_in, small2_in,
    quarters, p_ref, activated, pre_grad,
    t_send, t_recv, d_send, d_recv, local_sem,
):
    me_d = lax.axis_index("dp")
    me_t = lax.axis_index("tensor")
    rows, quarter = x_ref.shape
    width = quarter * n_t
    head_count = wq_ref.shape[1] // DH
    scale = DH ** (-0.5)
    bucket_count = table_ref.shape[0]
    total_slots = n_dp * pad

    barrier = pltpu.get_barrier_semaphore()
    for k in range(1, n_t):
        pl.semaphore_signal(
            barrier, inc=1, device_id=(me_d, lax.rem(me_t + k, n_t)), device_id_type=MESH
        )

    def greet(k, carry):
        pl.semaphore_signal(
            barrier, inc=1, device_id=(lax.rem(me_d + k, n_dp), me_t), device_id_type=MESH
        )
        return carry

    lax.fori_loop(1, n_dp, greet, 0)
    pl.semaphore_wait(barrier, n_t - 1 + n_dp - 1)

    def over_tensor(phase, source, target):
        copies = []
        for k in range(1, n_t):
            peer = lax.rem(me_t + k, n_t)
            copy = pltpu.make_async_remote_copy(
                src_ref=source(peer),
                dst_ref=target,
                send_sem=t_send.at[phase, k],
                recv_sem=t_recv.at[phase, k],
                device_id=(me_d, peer),
                device_id_type=MESH,
            )
            copy.start()
            copies.append(copy)
        return copies

    def finish(copies):
        for copy in copies:
            copy.wait()

    def dp_copy(phase, k, source, target, peer):
        return pltpu.make_async_remote_copy(
            src_ref=source(peer),
            dst_ref=target,
            send_sem=d_send.at[phase, k],
            recv_sem=d_recv.at[phase, k],
            device_id=(peer, me_t),
            device_id_type=MESH,
        )

    def dp_start(phase, source, target):
        def body(k, carry):
            dp_copy(phase, k, source, target, lax.rem(me_d + k, n_dp)).start()
            return carry

        lax.fori_loop(1, n_dp, body, 0)

    def dp_wait(phase, source, target):
        def body(k, carry):
            dp_copy(phase, k, source, target, lax.rem(me_d + k, n_dp)).wait()
            return carry

        lax.fori_loop(1, n_dp, body, 0)

    xs[me_t, 0] = x_ref[...]
    xs[me_t, 1] = dy_ref[...]
    gs[me_t] = jnp.broadcast_to(gain1_ref[...].astype(F32), (16, quarter)).astype(BF16)
    first = over_tensor(0, lambda p: xs.at[me_t], xs.at[me_t])
    first += over_tensor(1, lambda p: gs.at[me_t], gs.at[me_t])

    first_len = lens_ref[0]
    both_len = first_len + lens_ref[1]
    row_col = iota((rows, 1), 0)
    row_row = iota((1, rows), 1)

    def segment_of(position):
        return jnp.where(position < first_len, 0, jnp.where(position < both_len, 1, 2))

    live = (row_col < both_len).astype(F32)
    at_i = iota((rows, rows), 0)
    at_j = iota((rows, rows), 1)
    allowed = (at_i >= at_j) & (segment_of(row_col) == segment_of(row_row))
    eye = at_i == at_j
    flip = (lax.rem(at_i + at_j, rows) == 0).astype(F32).astype(BF16)
    chosen = (routes_ref[...] == iota((rows, n_dp), 1)).astype(F32)
    picked = chosen * live
    earlier = dot((at_j < at_i).astype(F32).astype(BF16), picked.astype(BF16))
    rank = jnp.sum(picked * earlier, axis=1, keepdims=True)
    slot = routes_ref[...].astype(F32) * pad + rank
    slot = jnp.where(live > 0, slot, -1.0)
    unpack = (slot == iota((rows, total_slots), 1).astype(F32)).astype(F32).astype(BF16)
    bucket_hot = (iota((bucket_count, rows), 0) == buckets_ref[...]).astype(F32)
    offset_bias = dot(table_ref[...], dot(bucket_hot.astype(BF16), flip).astype(BF16), 0, 0)

    finish(first)
    x_full = jnp.concatenate([xs[q, 0].astype(F32) for q in range(n_t)], axis=1)
    dy_full = jnp.concatenate([xs[q, 1].astype(F32) for q in range(n_t)], axis=1)
    gain1 = jnp.concatenate([gs[q].astype(F32)[0:1] for q in range(n_t)], axis=1)
    inv_one = lax.rsqrt(jnp.mean(x_full * x_full, axis=1, keepdims=True) + EPSILON)
    normed_one = (x_full * inv_one * gain1).astype(BF16)
    query = dot(normed_one, wq_ref[...]).astype(BF16)
    key = dot(normed_one, wk_ref[...]).astype(BF16)
    value = dot(normed_one, wv_ref[...]).astype(BF16)

    def head(values, h):
        return values[:, h * DH : (h + 1) * DH]

    outs = []
    attn_part = jnp.zeros((rows, width), F32)
    for h in range(head_count):
        bias = jnp.broadcast_to(offset_bias[h : h + 1], (rows, rows))
        bias = pltpu.roll(bias, 0, 1, stride=1, stride_axis=0)
        scores = dot(head(query, h), head(key, h), 1, 1) * scale + bias
        scores = jnp.where(allowed, scores, NEGATIVE)
        weights = jnp.exp(scores - jnp.max(scores, axis=1, keepdims=True))
        weights = weights / jnp.sum(weights, axis=1, keepdims=True)
        p_ref[h] = weights
        outs.append(dot(weights.astype(BF16), head(value, h)).astype(BF16))
        attn_part += dot(outs[h], wo_ref[h * DH : (h + 1) * DH])

    share = rows // n_t
    a_send[...] = attn_part.astype(BF16).reshape(n_t, share, width)
    a_recv[me_t] = a_send[me_t]
    finish(over_tensor(2, lambda p: a_send.at[p], a_recv.at[me_t]))
    a_total = a_recv[0].astype(F32)
    for q in range(1, n_t):
        a_total += a_recv[q].astype(F32)
    a_sum[me_t] = a_total.astype(BF16)
    finish(over_tensor(3, lambda p: a_sum.at[me_t], a_sum.at[me_t]))
    hidden = x_full + live * a_sum[...].reshape(rows, width).astype(F32)
    inv_two = lax.rsqrt(jnp.mean(hidden * hidden, axis=1, keepdims=True) + EPSILON)
    gain2 = gain2_ref[...].astype(F32)
    normal_two = hidden * inv_two
    normed_two = (normal_two * gain2).astype(BF16)
    logits = dot(normed_two, wr_ref[...])
    probs = jnp.exp(logits - jnp.max(logits, axis=1, keepdims=True))
    probs = probs / jnp.sum(probs, axis=1, keepdims=True)
    gate = jnp.sum(probs * chosen, axis=1, keepdims=True)
    moe_grad = (live * gate * dy_full).astype(BF16)

    sent[:, 0] = dot(unpack, normed_two, 0, 0).astype(BF16).reshape(n_dp, pad, width)
    sent[:, 1] = dot(unpack, moe_grad, 0, 0).astype(BF16).reshape(n_dp, pad, width)
    arrived[me_d] = sent[me_d]
    dispatch = (0, lambda p: sent.at[p], arrived.at[me_d])
    dp_start(*dispatch)
    for q in range(n_t):
        quarters[q] = hidden[:, q * quarter : (q + 1) * quarter]
    dp_wait(*dispatch)
    root = math.sqrt(2.0 / math.pi)
    step = total_slots if total_slots <= 512 else 256
    for begin in range(0, total_slots, step):
        span = slice(begin, begin + step)
        sources = slice(begin // pad, (begin + step) // pad)
        pre = dot(arrived[sources, 0].reshape(step, width), win_ref[0])
        square = pre * pre
        bent = jnp.tanh(root * (pre + 0.044715 * square * pre))
        activated[span] = (0.5 * pre * (1.0 + bent)).astype(BF16)
        slope = 0.5 * (1.0 + bent) + 0.5 * pre * (1.0 - bent * bent) * root * (
            1.0 + 3 * 0.044715 * square
        )
        wide = dot(activated[span], wout_ref[0])
        for q in range(n_t):
            parts[q, 0, span] = wide[:, q * quarter : (q + 1) * quarter].astype(BF16)
        act_grad = dot(arrived[sources, 1].reshape(step, width), wout_ref[0], 1, 1)
        pre_grad[span] = (act_grad * slope).astype(BF16)
        wide = dot(pre_grad[span], win_ref[0], 1, 1)
        for q in range(n_t):
            parts[q, 1, span] = wide[:, q * quarter : (q + 1) * quarter].astype(BF16)
    parts_in[me_t] = parts[me_t]
    shares = over_tensor(4, lambda p: parts.at[p], parts_in.at[me_t])
    dwout_ref[0] = dot(activated[...], arrived[:, 1].reshape(total_slots, width), 0, 0)
    dwin_ref[0] = dot(arrived[:, 0].reshape(total_slots, width), pre_grad[...], 0, 0)
    finish(shares)
    for s in range(2):
        total = parts_in[0, s].astype(F32)
        for q in range(1, n_t):
            total += parts_in[q, s].astype(F32)
        back[:, s] = total.astype(BF16).reshape(n_dp, pad, quarter)

    back_in[me_d] = back[me_d]
    home = (1, lambda p: back.at[p], back_in.at[me_d])
    dp_start(*home)
    dp_wait(*home)
    moe_quarter = dot(unpack, back_in[:, 0].reshape(total_slots, quarter))
    eg_all[me_t] = dot(unpack, back_in[:, 1].reshape(total_slots, quarter)).astype(BF16)

    def to_row(column):
        return jnp.sum(jnp.where(eye, column, 0.0), axis=0, keepdims=True)

    def to_column(line):
        return jnp.sum(jnp.where(eye, line, 0.0), axis=1, keepdims=True)

    gate_part = jnp.sum(xs[me_t, 1].astype(F32) * moe_quarter, axis=1, keepdims=True)
    row_part[...] = jnp.broadcast_to(to_row(gate_part), (8, rows))
    row_in[me_t] = row_part[...]
    sixth = over_tensor(5, lambda p: eg_all.at[me_t], eg_all.at[me_t])
    sixth += over_tensor(6, lambda p: row_part, row_in.at[me_t])
    out_ref[...] = (quarters[me_t] + live * gate * moe_quarter).astype(BF16)
    finish(sixth)
    row_total = row_in[0]
    for q in range(1, n_t):
        row_total += row_in[q]
    gate_grad = live * to_column(row_total[0:1])
    expert_grad = jnp.concatenate([eg_all[q].astype(F32) for q in range(n_t)], axis=1)
    logit_grad = (gate_grad * gate * (chosen - probs)).astype(BF16)
    two_grad = expert_grad + dot(logit_grad, wr_ref[...], 1, 1)
    small1[0:8] = jnp.broadcast_to(
        jnp.sum(two_grad * normal_two, axis=0, keepdims=True), (8, width)
    ).astype(BF16)
    small1[8 : 8 + n_dp] = dot(logit_grad, normed_two, 0, 0).astype(BF16)
    if 8 + n_dp < small1.shape[0]:
        small1[8 + n_dp :] = jnp.zeros((small1.shape[0] - 8 - n_dp, width), BF16)
    small1_in[me_d] = small1[...]
    small_one = (2, lambda p: small1, small1_in.at[me_d])
    dp_start(*small_one)
    scaled_two = two_grad * gain2
    hidden_grad = dy_full + inv_two * (
        scaled_two - normal_two * jnp.mean(scaled_two * normal_two, axis=1, keepdims=True)
    )
    attn_grad = (live * hidden_grad).astype(BF16)
    for q in range(n_t):
        quarters[q] = hidden_grad[:, q * quarter : (q + 1) * quarter]
    heads_grad = dot(attn_grad, wo_ref[...], 1, 1).astype(BF16)

    own = head_count * DH
    one_grad = jnp.zeros((rows, width), F32)
    small2[...] = jnp.zeros(small2.shape, F32)
    for h in range(head_count):
        lo = h * DH
        grads[3 * own + lo : 3 * own + lo + DH] = dot(outs[h], attn_grad, 0, 0).astype(BF16)
        weights = p_ref[h]
        grad_h = head(heads_grad, h)
        weight_grad = dot(grad_h, head(value, h), 1, 1)
        score_grad = (
            weights * (weight_grad - jnp.sum(weights * weight_grad, axis=1, keepdims=True))
        ).astype(BF16)
        query_grad = (dot(score_grad, head(key, h)) * scale).astype(BF16)
        key_grad = (dot(score_grad, head(query, h), 0, 0) * scale).astype(BF16)
        value_grad = dot(weights.astype(BF16), grad_h, 0, 0).astype(BF16)
        for at, (grad, w_ref) in enumerate(
            ((query_grad, wq_ref), (key_grad, wk_ref), (value_grad, wv_ref))
        ):
            grads[at * own + lo : at * own + lo + DH] = dot(grad, normed_one, 0, 0).astype(BF16)
            one_grad += dot(grad, w_ref[:, lo : lo + DH], 1, 1)
        diagonal = pltpu.roll(dot(score_grad, flip), 0, 1, stride=1, stride_axis=0)
        small2[h : h + 1] = jnp.sum(diagonal, axis=0, keepdims=True)

    chunk = grads_in.shape[1]
    owners = width // chunk

    def block(ref, index):
        return ref.at[pl.ds(pl.multiple_of(index * chunk, 16), chunk)]

    def guarded(condition, action):
        if owners == n_dp:
            action()
        else:
            pl.when(condition)(action)

    def scatter_copy(k, peer):
        return pltpu.make_async_remote_copy(
            src_ref=block(grads, peer),
            dst_ref=grads_in.at[me_d],
            send_sem=d_send.at[3, k],
            recv_sem=d_recv.at[3, k],
            device_id=(peer, me_t),
            device_id_type=MESH,
        )

    def scatter_start(k, carry):
        peer = lax.rem(me_d + k, n_dp)
        guarded(peer < owners, lambda: scatter_copy(k, peer).start())
        return carry

    lax.fori_loop(1, n_dp, scatter_start, 0)

    normal_one = x_full * inv_one
    row_sum = jnp.sum(one_grad * gain1 * normal_one, axis=1, keepdims=True)
    row2_part[...] = jnp.broadcast_to(to_row(row_sum), (8, rows))
    row2_in[me_t] = row2_part[...]
    for q in range(n_t):
        one_send[q] = one_grad[:, q * quarter : (q + 1) * quarter].astype(BF16)
    one_in[me_t] = one_send[me_t]
    eighth = over_tensor(7, lambda p: one_send.at[p], one_in.at[me_t])
    eighth += over_tensor(8, lambda p: row2_part, row2_in.at[me_t])
    finish(eighth)
    row_total = row2_in[0]
    one_part = one_in[0].astype(F32)
    for q in range(1, n_t):
        row_total += row2_in[q]
        one_part += one_in[q].astype(F32)
    row_mean = to_column(row_total[0:1]) / width
    normal_part = x_ref[...].astype(F32) * inv_one
    scaled_part = one_part * gain1_ref[...].astype(F32)
    dx_ref[...] = quarters[me_t] + inv_one * (scaled_part - normal_part * row_mean)
    gain_row = jnp.sum(one_part * normal_part, axis=0, keepdims=True)
    small2[head_count : head_count + 1, 0:quarter] = gain_row
    small2_in[me_d] = small2[...]
    small_two = (4, lambda p: small2, small2_in.at[me_d])
    dp_start(*small_two)

    def scatter_wait(k, carry):
        peer = lax.rem(me_d + k, n_dp)
        guarded(peer < owners, lambda: scatter_copy(k, peer).wait_send())
        guarded(me_d < owners, lambda: scatter_copy(k, peer).wait_recv())
        return carry

    lax.fori_loop(1, n_dp, scatter_wait, 0)

    def own_sum():
        grads_in[me_d] = block(grads, me_d)[...]
        total = grads_in[0].astype(F32)
        for d in range(1, n_dp):
            total += grads_in[d].astype(F32)
        block(grads_all, me_d)[...] = total.astype(BF16)

    guarded(me_d < owners, own_sum)

    def gather_copy(k, peer):
        return pltpu.make_async_remote_copy(
            src_ref=block(grads_all, me_d),
            dst_ref=block(grads_all, me_d),
            send_sem=d_send.at[5, k],
            recv_sem=d_recv.at[5, k],
            device_id=(peer, me_t),
            device_id_type=MESH,
        )

    def gather_start(k, carry):
        peer = lax.rem(me_d + k, n_dp)
        guarded(me_d < owners, lambda: gather_copy(k, peer).start())
        return carry

    lax.fori_loop(1, n_dp, gather_start, 0)

    dp_wait(*small_one)
    dp_wait(*small_two)
    small = small1_in[0].astype(F32)
    other = small2_in[0]
    for d in range(1, n_dp):
        small += small1_in[d].astype(F32)
        other += small2_in[d]
    dgain2_ref[...] = small[0:1]
    dwr_ref[...] = small[8 : 8 + n_dp]
    dgain1_ref[...] = other[head_count : head_count + 1, 0:quarter]
    for h in range(head_count):
        dtable_ref[:, h : h + 1] = jnp.sum(
            bucket_hot * other[h : h + 1], axis=1, keepdims=True
        )

    def gather_wait(k, carry):
        peer = lax.rem(me_d + k, n_dp)
        source = lax.rem(me_d + n_dp - k, n_dp)
        guarded(me_d < owners, lambda: gather_copy(k, peer).wait_send())

        def arrive():
            pltpu.make_async_remote_copy(
                src_ref=block(grads_all, source),
                dst_ref=block(grads_all, source),
                send_sem=d_send.at[5, k],
                recv_sem=d_recv.at[5, k],
                device_id=(peer, me_t),
                device_id_type=MESH,
            ).wait_recv()

        guarded(source < owners, arrive)
        return carry

    lax.fori_loop(1, n_dp, gather_wait, 0)
    for at, ref in enumerate((dwq_ref, dwk_ref, dwv_ref)):
        ref[...] = jnp.transpose(grads_all[at * own : (at + 1) * own].astype(F32))
    dwo_ref[...] = grads_all[3 * own :].astype(F32)


def on_device(
    activations, output_grad, seq_lengths, routes, buckets, norm1_gain, w_query, w_key, w_value,
    w_output, bias_table, norm2_gain, w_router, w_in, w_out,
):
    rows, quarter = activations.shape
    n_t = lax.axis_size("tensor")
    n_dp = lax.axis_size("dp")
    width = quarter * n_t
    own = w_query.shape[1]
    heads = own // DH
    slots = max(2, 9 * rows // (8 * n_dp))
    pad = -(-slots // 16) * 16
    chunk = max(16, width // n_dp)
    inner = w_in.shape[2]
    small_rows = -(-(8 + n_dp) // 16) * 16
    vmem = pl.BlockSpec(memory_space=pltpu.VMEM)
    smem = pl.BlockSpec(memory_space=pltpu.SMEM)

    def out(shape, dtype=F32):
        return jax.ShapeDtypeStruct(shape, dtype)

    results = pl.pallas_call(
        functools.partial(kernel, n_dp, n_t, slots, pad),
        out_shape=(
            out((rows, quarter), BF16),
            out((rows, quarter)),
            out((1, quarter)),
            out((width, own)),
            out((width, own)),
            out((width, own)),
            out((own, width)),
            out((bias_table.shape[0], heads)),
            out((1, width)),
            out((n_dp, width)),
            out((1, width, inner)),
            out((1, inner, width)),
        ),
        in_specs=[smem] + [vmem] * 14,
        out_specs=(vmem,) * 12,
        scratch_shapes=[
            pltpu.VMEM((n_t, 2, rows, quarter), BF16),
            pltpu.VMEM((n_t, 16, quarter), BF16),
            pltpu.VMEM((n_t, rows // n_t, width), BF16),
            pltpu.VMEM((n_t, rows // n_t, width), BF16),
            pltpu.VMEM((n_t, rows // n_t, width), BF16),
            pltpu.VMEM((n_dp, 2, pad, width), BF16),
            pltpu.VMEM((n_dp, 2, pad, width), BF16),
            pltpu.VMEM((n_t, 2, n_dp * pad, quarter), BF16),
            pltpu.VMEM((n_t, 2, n_dp * pad, quarter), BF16),
            pltpu.VMEM((n_dp, 2, pad, quarter), BF16),
            pltpu.VMEM((n_dp, 2, pad, quarter), BF16),
            pltpu.VMEM((n_t, rows, quarter), BF16),
            pltpu.VMEM((8, rows), F32),
            pltpu.VMEM((n_t, 8, rows), F32),
            pltpu.VMEM((n_t, rows, quarter), BF16),
            pltpu.VMEM((n_t, rows, quarter), BF16),
            pltpu.VMEM((8, rows), F32),
            pltpu.VMEM((n_t, 8, rows), F32),
            pltpu.VMEM((width, width), BF16),
            pltpu.VMEM((n_dp, chunk, width), BF16),
            pltpu.VMEM((width, width), BF16),
            pltpu.VMEM((small_rows, width), BF16),
            pltpu.VMEM((8, rows), F32),
            pltpu.VMEM((n_dp, small_rows, width), BF16),
            pltpu.VMEM((n_dp, 8, rows), F32),
            pltpu.VMEM((n_t, rows, quarter), F32),
            pltpu.VMEM((heads, rows, rows), F32),
            pltpu.VMEM((n_dp * pad, inner), BF16),
            pltpu.VMEM((n_dp * pad, inner), BF16),
            pltpu.SemaphoreType.DMA((9, n_t)),
            pltpu.SemaphoreType.DMA((9, n_t)),
            pltpu.SemaphoreType.DMA((6, n_dp)),
            pltpu.SemaphoreType.DMA((6, n_dp)),
            pltpu.SemaphoreType.DMA,
        ],
        compiler_params=pltpu.CompilerParams(
            collective_id=0, has_side_effects=True, vmem_limit_bytes=60 * 1024 * 1024
        ),
    )(
        seq_lengths, activations, output_grad, routes, buckets.reshape(1, rows),
        norm1_gain.reshape(1, quarter), w_query, w_key, w_value, w_output, bias_table,
        norm2_gain.reshape(1, width), w_router, w_in, w_out,
    )
    r = list(results)
    r[2] = r[2].reshape(quarter)
    r[8] = r[8].reshape(width)
    r[9] = jnp.transpose(r[9])
    return tuple(r)


def solution(mesh):
    in_specs = (
        P("dp", "tensor"),
        P("dp", "tensor"),
        P("dp"),
        P("dp", None),
        P(),
        P("tensor"),
        P(None, "tensor"),
        P(None, "tensor"),
        P(None, "tensor"),
        P("tensor", None),
        P(None, "tensor"),
        P(),
        P(),
        P("dp", None, "tensor"),
        P("dp", "tensor", None),
    )
    out_specs = (
        P("dp", "tensor"),
        P("dp", "tensor"),
        P("tensor"),
        P(None, "tensor"),
        P(None, "tensor"),
        P(None, "tensor"),
        P("tensor", None),
        P(None, "tensor"),
        P(),
        P(),
        P("dp", None, "tensor"),
        P("dp", "tensor", None),
    )
    return jax.shard_map(
        on_device, mesh=mesh, in_specs=in_specs, out_specs=out_specs, check_vma=False
    )
```

```python
import functools
import math

import jax
import jax.numpy as jnp
from jax import lax
from jax.experimental import pallas as pl
from jax.experimental.pallas import tpu as pltpu
from jax.sharding import PartitionSpec as P

DH = 64
EPSILON = 1e-06
NEGATIVE = -1e30
F32 = jnp.float32
BF16 = jnp.bfloat16
MESH = pl.DeviceIdType.MESH


def dot(left, right, left_axis=1, right_axis=0):
    return lax.dot_general(
        left, right, (((left_axis,), (right_axis,)), ((), ())), preferred_element_type=F32
    )


def iota(shape, axis):
    return lax.broadcasted_iota(jnp.int32, shape, axis)


def kernel(
    n_dp, n_t, slots, pad,
    lens_ref, x_ref, dy_ref, routes_ref, buckets_ref, gain1_ref, wq_ref, wk_ref, wv_ref, wo_ref,
    table_ref, gain2_ref, wr_ref, win_ref, wout_ref,
    out_ref, dx_ref, dgain1_ref, dwq_ref, dwk_ref, dwv_ref, dwo_ref, dtable_ref, dgain2_ref,
    dwr_ref, dwin_ref, dwout_ref,
    xs, gs, a_send, a_recv, a_sum, sent, arrived, parts, parts_in, back, back_in,
    eg_all, row_part, row_in, one_send, one_in, row2_part, row2_in,
    grads, pair_in, pair_sum, grads_in, grads_all, small1, small2, small1_in, small2_in,
    quarters, p_ref, activated, pre_grad,
    t_send, t_recv, d_send, d_recv, p_send, p_recv, z_send, z_recv, g_send, g_recv, f_send,
):
    me_d = lax.axis_index("dp")
    me_t = lax.axis_index("tensor")
    quarter, rows = x_ref.shape
    width = quarter * n_t
    head_count = wq_ref.shape[0] // DH
    scale = DH ** (-0.5)
    bucket_count = table_ref.shape[1]
    total_slots = n_dp * pad

    barrier = pltpu.get_barrier_semaphore()
    for k in range(1, n_t):
        pl.semaphore_signal(
            barrier, inc=1, device_id=(me_d, lax.rem(me_t + k, n_t)), device_id_type=MESH
        )

    def greet(k, carry):
        pl.semaphore_signal(
            barrier, inc=1, device_id=(lax.rem(me_d + k, n_dp), me_t), device_id_type=MESH
        )
        return carry

    lax.fori_loop(1, n_dp, greet, 0)
    pl.semaphore_wait(barrier, n_t - 1 + n_dp - 1)

    def over_tensor(phase, source, target):
        copies = []
        for k in range(1, n_t):
            peer = lax.rem(me_t + k, n_t)
            copy = pltpu.make_async_remote_copy(
                src_ref=source(peer),
                dst_ref=target,
                send_sem=t_send.at[phase, k],
                recv_sem=t_recv.at[phase, k],
                device_id=(me_d, peer),
                device_id_type=MESH,
            )
            copy.start()
            copies.append(copy)
        return copies

    def finish(copies):
        for copy in copies:
            copy.wait()

    def dp_copy(phase, k, source, target, peer):
        return pltpu.make_async_remote_copy(
            src_ref=source(peer),
            dst_ref=target,
            send_sem=d_send.at[phase, k],
            recv_sem=d_recv.at[phase, k],
            device_id=(peer, me_t),
            device_id_type=MESH,
        )

    def dp_start(phase, source, target):
        def body(k, carry):
            dp_copy(phase, k, source, target, lax.rem(me_d + k, n_dp)).start()
            return carry

        lax.fori_loop(1, n_dp, body, 0)

    def dp_wait(phase, source, target):
        def body(k, carry):
            dp_copy(phase, k, source, target, lax.rem(me_d + k, n_dp)).wait()
            return carry

        lax.fori_loop(1, n_dp, body, 0)

    xs[me_t, 0] = x_ref[...]
    xs[me_t, 1] = dy_ref[...]
    gs[me_t] = jnp.broadcast_to(gain1_ref[...].astype(F32), (16, quarter)).astype(BF16)
    first = over_tensor(0, lambda p: xs.at[me_t], xs.at[me_t])
    first += over_tensor(1, lambda p: gs.at[me_t], gs.at[me_t])

    first_len = lens_ref[0]
    both_len = first_len + lens_ref[1]
    row_col = iota((rows, 1), 0)
    row_row = iota((1, rows), 1)

    def segment_of(position):
        return jnp.where(position < first_len, 0, jnp.where(position < both_len, 1, 2))

    live = (row_col < both_len).astype(F32)
    at_i = iota((rows, rows), 0)
    at_j = iota((rows, rows), 1)
    allowed = (at_i >= at_j) & (segment_of(row_col) == segment_of(row_row))
    eye = at_i == at_j
    flip = (lax.rem(at_i + at_j, rows) == 0).astype(F32).astype(BF16)
    live_row = (row_row < both_len).astype(F32)

    def to_row(column):
        return jnp.sum(jnp.where(eye, column, 0.0), axis=0, keepdims=True)

    def to_column(line):
        return jnp.sum(jnp.where(eye, line, 0.0), axis=1, keepdims=True)

    routes = to_column(routes_ref[...].astype(F32))
    chosen = (routes.astype(jnp.int32) == iota((rows, n_dp), 1)).astype(F32)
    picked = chosen * live
    earlier = dot((at_j < at_i).astype(F32).astype(BF16), picked.astype(BF16))
    rank = jnp.sum(picked * earlier, axis=1, keepdims=True)
    slot = routes * pad + rank
    slot = jnp.where(live > 0, slot, -1.0)
    unpack = (slot == iota((rows, total_slots), 1).astype(F32)).astype(F32).astype(BF16)
    bucket_hot = (iota((bucket_count, rows), 0) == buckets_ref[...]).astype(F32)
    offset_bias = dot(table_ref[...], dot(bucket_hot.astype(BF16), flip).astype(BF16))

    finish(first)
    x_full = jnp.transpose(xs[:, 0].reshape(width, rows).astype(F32))
    dy_full = jnp.transpose(xs[:, 1].reshape(width, rows).astype(F32))
    gain1 = jnp.concatenate([gs[q].astype(F32)[0:1] for q in range(n_t)], axis=1)
    inv_one = lax.rsqrt(jnp.mean(x_full * x_full, axis=1, keepdims=True) + EPSILON)
    normed_one = (x_full * inv_one * gain1).astype(BF16)
    query = dot(normed_one, wq_ref[...], 1, 1).astype(BF16)
    key = dot(normed_one, wk_ref[...], 1, 1).astype(BF16)
    value = dot(normed_one, wv_ref[...], 1, 1).astype(BF16)

    def head(values, h):
        return values[:, h * DH : (h + 1) * DH]

    outs = []
    attn_part = jnp.zeros((rows, width), F32)
    for h in range(head_count):
        bias = jnp.broadcast_to(offset_bias[h : h + 1], (rows, rows))
        bias = pltpu.roll(bias, 0, 1, stride=1, stride_axis=0)
        scores = dot(head(query, h), head(key, h), 1, 1) * scale + bias
        scores = jnp.where(allowed, scores, NEGATIVE)
        weights = jnp.exp(scores - jnp.max(scores, axis=1, keepdims=True))
        weights = weights / jnp.sum(weights, axis=1, keepdims=True)
        p_ref[h] = weights
        outs.append(dot(weights.astype(BF16), head(value, h)).astype(BF16))
        attn_part += dot(outs[h], wo_ref[h * DH : (h + 1) * DH])

    share = rows // n_t
    a_send[...] = attn_part.astype(BF16).reshape(n_t, share, width)
    a_recv[me_t] = a_send[me_t]
    finish(over_tensor(2, lambda p: a_send.at[p], a_recv.at[me_t]))
    a_total = a_recv[0].astype(F32)
    for q in range(1, n_t):
        a_total += a_recv[q].astype(F32)
    a_sum[me_t] = a_total.astype(BF16)
    finish(over_tensor(3, lambda p: a_sum.at[me_t], a_sum.at[me_t]))
    hidden = x_full + live * a_sum[...].reshape(rows, width).astype(F32)
    inv_two = lax.rsqrt(jnp.mean(hidden * hidden, axis=1, keepdims=True) + EPSILON)
    gain2 = gain2_ref[...].astype(F32)
    normal_two = hidden * inv_two
    normed_two = (normal_two * gain2).astype(BF16)
    logits = dot(normed_two, wr_ref[...], 1, 1)
    probs = jnp.exp(logits - jnp.max(logits, axis=1, keepdims=True))
    probs = probs / jnp.sum(probs, axis=1, keepdims=True)
    gate = jnp.sum(probs * chosen, axis=1, keepdims=True)
    moe_grad = (live * gate * dy_full).astype(BF16)

    sent[:, 0] = dot(unpack, normed_two, 0, 0).astype(BF16).reshape(n_dp, pad, width)
    sent[:, 1] = dot(unpack, moe_grad, 0, 0).astype(BF16).reshape(n_dp, pad, width)
    arrived[me_d] = sent[me_d]
    dispatch = (0, lambda p: sent.at[p], arrived.at[me_d])
    dp_start(*dispatch)
    quarters[...] = jnp.transpose(hidden).reshape(n_t, quarter, rows)
    dp_wait(*dispatch)
    root = math.sqrt(2.0 / math.pi)
    step = total_slots if total_slots <= 512 else 256
    for begin in range(0, total_slots, step):
        span = slice(begin, begin + step)
        sources = slice(begin // pad, (begin + step) // pad)
        pre = dot(arrived[sources, 0].reshape(step, width), win_ref[0])
        square = pre * pre
        bent = jnp.tanh(root * (pre + 0.044715 * square * pre))
        activated[span] = (0.5 * pre * (1.0 + bent)).astype(BF16)
        slope = 0.5 * (1.0 + bent) + 0.5 * pre * (1.0 - bent * bent) * root * (
            1.0 + 3 * 0.044715 * square
        )
        wide = dot(wout_ref[0], activated[span], 0, 1).astype(BF16)
        parts[:, 0, :, span] = wide.reshape(n_t, quarter, step)
        act_grad = dot(arrived[sources, 1].reshape(step, width), wout_ref[0], 1, 1)
        pre_grad[span] = (act_grad * slope).astype(BF16)
        wide = dot(win_ref[0], pre_grad[span], 1, 1).astype(BF16)
        parts[:, 1, :, span] = wide.reshape(n_t, quarter, step)
    parts_in[me_t] = parts[me_t]
    shares = over_tensor(4, lambda p: parts.at[p], parts_in.at[me_t])
    dwout_ref[0] = dot(activated[...], arrived[:, 1].reshape(total_slots, width), 0, 0)
    dwin_ref[0] = dot(arrived[:, 0].reshape(total_slots, width), pre_grad[...], 0, 0)
    finish(shares)
    for s in range(2):
        total = parts_in[0, s].astype(F32)
        for q in range(1, n_t):
            total += parts_in[q, s].astype(F32)
        back[:, s] = jnp.transpose(total).astype(BF16).reshape(n_dp, pad, quarter)

    back_in[me_d] = back[me_d]
    home = (1, lambda p: back.at[p], back_in.at[me_d])
    dp_start(*home)
    dp_wait(*home)
    moe_quarter = dot(back_in[:, 0].reshape(total_slots, quarter), unpack, 0, 1)
    eg_all[me_t] = dot(back_in[:, 1].reshape(total_slots, quarter), unpack, 0, 1).astype(BF16)

    gate_part = jnp.sum(xs[me_t, 1].astype(F32) * moe_quarter, axis=0, keepdims=True)
    row_part[...] = jnp.broadcast_to(gate_part, (8, rows))
    row_in[me_t] = row_part[...]
    sixth = over_tensor(5, lambda p: eg_all.at[me_t], eg_all.at[me_t])
    sixth += over_tensor(6, lambda p: row_part, row_in.at[me_t])
    out_ref[...] = (quarters[me_t] + live_row * to_row(gate) * moe_quarter).astype(BF16)
    finish(sixth)
    row_total = row_in[0]
    for q in range(1, n_t):
        row_total += row_in[q]
    gate_grad = live * to_column(row_total[0:1])
    expert_grad = jnp.transpose(eg_all[...].reshape(width, rows).astype(F32))
    logit_grad = (gate_grad * gate * (chosen - probs)).astype(BF16)
    two_grad = expert_grad + dot(logit_grad, wr_ref[...])
    small1[0:8] = jnp.broadcast_to(
        jnp.sum(two_grad * normal_two, axis=0, keepdims=True), (8, width)
    ).astype(BF16)
    small1[8 : 8 + n_dp] = dot(logit_grad, normed_two, 0, 0).astype(BF16)
    if 8 + n_dp < small1.shape[0]:
        small1[8 + n_dp :] = jnp.zeros((small1.shape[0] - 8 - n_dp, width), BF16)
    small1_in[me_d] = small1[...]
    small_one = (2, lambda p: small1, small1_in.at[me_d])
    dp_start(*small_one)
    scaled_two = two_grad * gain2
    hidden_grad = dy_full + inv_two * (
        scaled_two - normal_two * jnp.mean(scaled_two * normal_two, axis=1, keepdims=True)
    )
    attn_grad = (live * hidden_grad).astype(BF16)
    quarters[...] = jnp.transpose(hidden_grad).reshape(n_t, quarter, rows)
    heads_grad = dot(attn_grad, wo_ref[...], 1, 1).astype(BF16)

    own = head_count * DH
    chunk = grads_in.shape[1]
    pairs = pair_in.shape[0]
    outer = n_dp // 2
    in_pair = lax.rem(me_d, 2)
    pair = me_d // 2
    mate = me_d + 1 - 2 * in_pair

    def block(ref, index):
        return ref.at[pl.ds(pl.multiple_of(index * chunk, 16), chunk)]

    def guarded(condition, action):
        if pairs == outer:
            action()
        else:
            pl.when(condition)(action)

    def to(source, target, send, recv, peer):
        return pltpu.make_async_remote_copy(
            src_ref=source, dst_ref=target, send_sem=send, recv_sem=recv,
            device_id=(peer, me_t), device_id_type=MESH,
        )

    def pair_copy(z):
        return to(
            block(grads, 2 * z + 1 - in_pair), pair_in.at[z], p_send.at[z], p_recv.at[z], mate
        )

    def outer_copy(z):
        return to(
            pair_sum.at[z], grads_in.at[pair], z_send.at[z], z_recv.at[pair], 2 * z + in_pair
        )

    def matrix(m):
        return range(m * (pairs // 4), (m + 1) * (pairs // 4))

    def pairs_start(m):
        for z in matrix(m):
            pair_copy(z).start()

    def pairs_pass(m):
        for z in matrix(m):
            pair_copy(z).wait()
            mine = block(grads, 2 * z + in_pair)[...].astype(F32)
            pair_sum[z] = (mine + pair_in[z].astype(F32)).astype(BF16)
            pl.when(pair != z)(outer_copy(z).start)

    def spans(h):
        return slice(h * DH, (h + 1) * DH)

    for h in range(head_count):
        lo = 3 * own + h * DH
        grads[lo : lo + DH] = dot(outs[h], attn_grad, 0, 0).astype(BF16)
    pairs_start(3)
    one_grad = jnp.zeros((rows, width), F32)
    small2[...] = jnp.zeros(small2.shape, F32)
    score_grads = []
    for h in range(head_count):
        weights = p_ref[h]
        grad_h = head(heads_grad, h)
        value_grad = dot(weights.astype(BF16), grad_h, 0, 0).astype(BF16)
        lo = 2 * own + h * DH
        grads[lo : lo + DH] = dot(value_grad, normed_one, 0, 0).astype(BF16)
        one_grad += dot(value_grad, wv_ref[spans(h)])
    pairs_start(2)
    for h in range(head_count):
        weights = p_ref[h]
        weight_grad = dot(head(heads_grad, h), head(value, h), 1, 1)
        score_grad = (
            weights * (weight_grad - jnp.sum(weights * weight_grad, axis=1, keepdims=True))
        ).astype(BF16)
        score_grads.append(score_grad)
        key_grad = (dot(score_grad, head(query, h), 0, 0) * scale).astype(BF16)
        lo = own + h * DH
        grads[lo : lo + DH] = dot(key_grad, normed_one, 0, 0).astype(BF16)
        one_grad += dot(key_grad, wk_ref[spans(h)])
    pairs_start(1)
    pairs_pass(3)
    for h in range(head_count):
        query_grad = (dot(score_grads[h], head(key, h)) * scale).astype(BF16)
        lo = h * DH
        grads[lo : lo + DH] = dot(query_grad, normed_one, 0, 0).astype(BF16)
        one_grad += dot(query_grad, wq_ref[spans(h)])
    pairs_start(0)
    pairs_pass(2)
    for h in range(head_count):
        diagonal = pltpu.roll(dot(score_grads[h], flip), 0, 1, stride=1, stride_axis=0)
        small2[h : h + 1] = jnp.sum(diagonal, axis=0, keepdims=True)

    normal_one = x_full * inv_one
    row_sum = jnp.sum(one_grad * gain1 * normal_one, axis=1, keepdims=True)
    row2_part[...] = jnp.broadcast_to(to_row(row_sum), (8, rows))
    row2_in[me_t] = row2_part[...]
    one_send[...] = jnp.transpose(one_grad).astype(BF16).reshape(n_t, quarter, rows)
    one_in[me_t] = one_send[me_t]
    eighth = over_tensor(7, lambda p: one_send.at[p], one_in.at[me_t])
    eighth += over_tensor(8, lambda p: row2_part, row2_in.at[me_t])
    pairs_pass(1)
    pairs_pass(0)
    finish(eighth)
    row_total = row2_in[0]
    one_part = one_in[0].astype(F32)
    for q in range(1, n_t):
        row_total += row2_in[q]
        one_part += one_in[q].astype(F32)
    row_mean = row_total[0:1] / width
    inv_row = to_row(inv_one)
    eye_quarter = iota((quarter, quarter), 0) == iota((quarter, quarter), 1)
    normal_part = x_ref[...].astype(F32) * inv_row
    gain_column = jnp.sum(
        jnp.where(eye_quarter, gain1_ref[...].astype(F32), 0.0), axis=1, keepdims=True
    )
    scaled_part = one_part * gain_column
    dx_ref[...] = quarters[me_t] + inv_row * (scaled_part - normal_part * row_mean)
    gain_sum = jnp.sum(one_part * normal_part, axis=1, keepdims=True)
    gain_row = jnp.sum(jnp.where(eye_quarter, gain_sum, 0.0), axis=0, keepdims=True)
    small2[head_count : head_count + 1, 0:quarter] = gain_row
    small2_in[me_d] = small2[...]
    small_two = (4, lambda p: small2, small2_in.at[me_d])
    dp_start(*small_two)

    for z in range(pairs):
        pl.when(pair != z)(outer_copy(z).wait_send)

    def own_sum():
        for k in range(1, outer):
            z = lax.rem(pair + k, outer)
            to(pair_sum.at[0], grads_in.at[z], z_send.at[0], z_recv.at[z], mate).wait_recv()
        grads_in[pair] = pair_sum[pair]
        total = grads_in[0].astype(F32)
        for z in range(1, outer):
            total += grads_in[z].astype(F32)
        block(grads_all, me_d)[...] = total.astype(BF16)

    def pass_block(index, send, peer):
        here = block(grads_all, index)
        return to(here, here, send, g_recv.at[index], peer)

    def own_copies():
        copies = [pass_block(me_d, g_send.at[0], mate)]
        for k in range(1, outer):
            peer = 2 * lax.rem(pair + k, outer) + in_pair
            copies.append(pass_block(me_d, g_send.at[k], peer))
        return copies

    def own_start():
        own_sum()
        for copy in reversed(own_copies()):
            copy.start()

    guarded(pair < pairs, own_start)

    def onward(k):
        source = lax.rem(pair + outer - k, outer)
        return source, pass_block(2 * source + in_pair, f_send.at[k], mate)

    def go_on(copy):
        copy.wait_recv()
        copy.start()

    for k in range(1, outer):
        source, copy = onward(k)
        guarded(source < pairs, functools.partial(go_on, copy))

    dp_wait(*small_one)
    dp_wait(*small_two)
    small = small1_in[0].astype(F32)
    other = small2_in[0]
    for d in range(1, n_dp):
        small += small1_in[d].astype(F32)
        other += small2_in[d]
    dgain2_ref[...] = small[0:1]
    dwr_ref[...] = small[8 : 8 + n_dp]
    dgain1_ref[...] = other[head_count : head_count + 1, 0:quarter]
    for h in range(head_count):
        sums = jnp.sum(bucket_hot * other[h : h + 1], axis=1, keepdims=True)
        corner = iota((bucket_count, bucket_count), 0) == iota((bucket_count, bucket_count), 1)
        dtable_ref[h : h + 1] = jnp.sum(jnp.where(corner, sums, 0.0), axis=0, keepdims=True)

    for z in range(pairs):
        pass_block(2 * z + 1 - in_pair, g_send.at[0], mate).wait_recv()

    def own_wait():
        for copy in own_copies():
            copy.wait_send()

    guarded(pair < pairs, own_wait)
    for k in range(1, outer):
        source, copy = onward(k)
        guarded(source < pairs, copy.wait_send)
    for at, ref in enumerate((dwq_ref, dwk_ref, dwv_ref)):
        ref[...] = grads_all[at * own : (at + 1) * own].astype(F32)
    dwo_ref[...] = grads_all[3 * own :].astype(F32)


def on_device(
    activations, output_grad, seq_lengths, routes, buckets, norm1_gain, w_query, w_key, w_value,
    w_output, bias_table, norm2_gain, w_router, w_in, w_out,
):
    rows, quarter = activations.shape
    n_t = lax.axis_size("tensor")
    n_dp = lax.axis_size("dp")
    width = quarter * n_t
    own = w_query.shape[1]
    heads = own // DH
    slots = max(2, 9 * rows // (8 * n_dp))
    pad = -(-slots // 16) * 16
    chunk = max(16, width // n_dp)
    inner = w_in.shape[2]
    pairs = width // chunk // 2
    small_rows = -(-(8 + n_dp) // 16) * 16
    vmem = pl.BlockSpec(memory_space=pltpu.VMEM)
    smem = pl.BlockSpec(memory_space=pltpu.SMEM)

    def out(shape, dtype=F32):
        return jax.ShapeDtypeStruct(shape, dtype)

    results = pl.pallas_call(
        functools.partial(kernel, n_dp, n_t, slots, pad),
        out_shape=(
            out((quarter, rows), BF16),
            out((quarter, rows)),
            out((1, quarter)),
            out((own, width)),
            out((own, width)),
            out((own, width)),
            out((own, width)),
            out((heads, bias_table.shape[0])),
            out((1, width)),
            out((n_dp, width)),
            out((1, width, inner)),
            out((1, inner, width)),
        ),
        in_specs=[smem] + [vmem] * 14,
        out_specs=(vmem,) * 12,
        scratch_shapes=[
            pltpu.VMEM((n_t, 2, quarter, rows), BF16),
            pltpu.VMEM((n_t, 16, quarter), BF16),
            pltpu.VMEM((n_t, rows // n_t, width), BF16),
            pltpu.VMEM((n_t, rows // n_t, width), BF16),
            pltpu.VMEM((n_t, rows // n_t, width), BF16),
            pltpu.VMEM((n_dp, 2, pad, width), BF16),
            pltpu.VMEM((n_dp, 2, pad, width), BF16),
            pltpu.VMEM((n_t, 2, quarter, n_dp * pad), BF16),
            pltpu.VMEM((n_t, 2, quarter, n_dp * pad), BF16),
            pltpu.VMEM((n_dp, 2, pad, quarter), BF16),
            pltpu.VMEM((n_dp, 2, pad, quarter), BF16),
            pltpu.VMEM((n_t, quarter, rows), BF16),
            pltpu.VMEM((8, rows), F32),
            pltpu.VMEM((n_t, 8, rows), F32),
            pltpu.VMEM((n_t, quarter, rows), BF16),
            pltpu.VMEM((n_t, quarter, rows), BF16),
            pltpu.VMEM((8, rows), F32),
            pltpu.VMEM((n_t, 8, rows), F32),
            pltpu.VMEM((width, width), BF16),
            pltpu.VMEM((pairs, chunk, width), BF16),
            pltpu.VMEM((pairs, chunk, width), BF16),
            pltpu.VMEM((n_dp // 2, chunk, width), BF16),
            pltpu.VMEM((width, width), BF16),
            pltpu.VMEM((small_rows, width), BF16),
            pltpu.VMEM((8, rows), F32),
            pltpu.VMEM((n_dp, small_rows, width), BF16),
            pltpu.VMEM((n_dp, 8, rows), F32),
            pltpu.VMEM((n_t, quarter, rows), F32),
            pltpu.VMEM((heads, rows, rows), F32),
            pltpu.VMEM((n_dp * pad, inner), BF16),
            pltpu.VMEM((n_dp * pad, inner), BF16),
            pltpu.SemaphoreType.DMA((9, n_t)),
            pltpu.SemaphoreType.DMA((9, n_t)),
            pltpu.SemaphoreType.DMA((6, n_dp)),
            pltpu.SemaphoreType.DMA((6, n_dp)),
            pltpu.SemaphoreType.DMA((pairs,)),
            pltpu.SemaphoreType.DMA((pairs,)),
            pltpu.SemaphoreType.DMA((pairs,)),
            pltpu.SemaphoreType.DMA((n_dp // 2,)),
            pltpu.SemaphoreType.DMA((n_dp // 2,)),
            pltpu.SemaphoreType.DMA((n_dp,)),
            pltpu.SemaphoreType.DMA((n_dp // 2,)),
        ],
        compiler_params=pltpu.CompilerParams(
            collective_id=0, has_side_effects=True, vmem_limit_bytes=60 * 1024 * 1024
        ),
    )(
        seq_lengths, activations.T, output_grad.T, routes.reshape(1, rows),
        buckets.reshape(1, rows), norm1_gain.reshape(1, quarter), w_query.T, w_key.T, w_value.T,
        w_output, bias_table.T, norm2_gain.reshape(1, width), w_router.T, w_in, w_out,
    )
    r = list(results)
    r[2] = r[2].reshape(quarter)
    r[8] = r[8].reshape(width)
    for at in (0, 1, 3, 4, 5, 7, 9):
        r[at] = jnp.transpose(r[at])
    return tuple(r)


def solution(mesh):
    in_specs = (
        P("dp", "tensor"),
        P("dp", "tensor"),
        P("dp"),
        P("dp", None),
        P(),
        P("tensor"),
        P(None, "tensor"),
        P(None, "tensor"),
        P(None, "tensor"),
        P("tensor", None),
        P(None, "tensor"),
        P(),
        P(),
        P("dp", None, "tensor"),
        P("dp", "tensor", None),
    )
    out_specs = (
        P("dp", "tensor"),
        P("dp", "tensor"),
        P("tensor"),
        P(None, "tensor"),
        P(None, "tensor"),
        P(None, "tensor"),
        P("tensor", None),
        P(None, "tensor"),
        P(),
        P(),
        P("dp", None, "tensor"),
        P("dp", "tensor", None),
    )
    return jax.shard_map(
        on_device, mesh=mesh, in_specs=in_specs, out_specs=out_specs, check_vma=False
    )
```
